32 devices in a mesh: section: 4 (over y, core), seq: 8 (over z, x).
Axes of the slice: x: 2, y: 2, z: 4, core: 2. Of those that a mesh axis runs over, the one named last changes fastest.
Arguments:
- activations: bfloat16 [4, 4096, 2048], P('section', 'seq'), may hold values from -6 to 6
- norm_gain: float32 [4, 2048], P('section'), may hold values from 0.5 to 1.5
- value_weight: bfloat16 [4, 2048, 1024], P('section'), may hold values from -0.125 to 0.125
- shared_weight: bfloat16 [4, 2048, 256], P('section'), may hold values from -0.125 to 0.125
- rate_weight: bfloat16 [4, 2048, 8], P('section'), may hold values from -0.125 to 0.125
- rate_bias: float32 [4, 8], P('section'), may hold values from -1 to 1
- decay_rate: float32 [4, 8], P('section'), may hold values from 0.00012207031 to 0.03
- level_table: float32 [4, 16, 13, 8], P('section'), may hold values from 0.25 to 2
- level_ids: int32 [4, 4096, 13], P('section', 'seq'), may hold values from 0 to 15
- out_gain: float32 [4, 1024], P('section'), may hold values from 0.5 to 1.5
- out_weight: bfloat16 [4, 1024, 2048], P('section'), may hold values from -0.1875 to 0.1875
Outputs:
- result: bfloat16 [4, 4096, 2048], P('section', 'seq')
The draws below stay inside these ranges and needn't reach their ends.
All inputs are finite; a program needn't handle non-finite values.
Results may differ from the reference program's by a relative error of at most 0.03.
Values may be sent and summed in bfloat16 or wider, within the bound.
A program may use at most 128 MiB of HBM per device.

```python
import math
import jax
import jax.numpy as jnp
from jax import lax

D = 2048
HW = 8
P_SIZE = 128
N = 128
BUCKETS = 16
TOK_DEV = 512
TOK_BITS = 9
SEQ_BITS = 3
LEVELS = 13
TOKENS = 4096
SECTIONS = 4
N_SEQ = 8


def with_ends(array, stream_key, smallest, high):
    longest = array.shape.index(max(array.shape))
    spots = []
    for shift in (0, 1):
        where = [jax.random.randint(jax.random.fold_in(stream_key, axis), (), 0, length) for axis, length in enumerate(array.shape)]
        where[longest] = (where[longest] + shift) % array.shape[longest]
        spots.append(tuple(where))
    return array.at[spots[0]].set(smallest).at[spots[1]].set(high)


def level_of(rng, dims, split, smallest, largest):
    def one(dim, shards_of):
        draws = jax.random.uniform(jax.random.fold_in(jax.random.fold_in(rng, 6), dim), (shards_of,), jnp.float32, smallest / len(split), largest / len(split))
        return jnp.repeat(jnp.exp(draws), dims[dim] // shards_of).reshape((-1,) + (1,) * (len(dims) - dim - 1))

    gain = one(*split[0])
    for cut in split[1:]:
        gain = gain * one(*cut)
    return gain


def centred(key, extent, deviation, bound, shards=(), kind=jnp.bfloat16):
    loudness = level_of(key, extent, shards, -0.22, 0.18) if shards else 1.0
    values = jax.random.normal(key, extent, jnp.float32) * deviation * loudness
    return jnp.minimum(jnp.maximum(values, -bound), bound).astype(kind)


def setup_inputs(seed: int = 0) -> dict:
    streams_of = jax.random.split(jax.random.key(seed), 12)
    return {
        "activations": centred(streams_of[0], (SECTIONS, TOKENS, D), 1.0, 6.0, ((0, 4), (1, 8))),
        "norm_gain": jnp.clip(1.0 + 0.1 * jax.random.normal(streams_of[1], (SECTIONS, D), jnp.float32), 0.5, 1.5),
        "value_weight": centred(streams_of[2], (SECTIONS, D, HW * P_SIZE), D ** -0.5, 0.125, ((0, 4),)),
        "shared_weight": centred(streams_of[3], (SECTIONS, D, 2 * N), D ** -0.5, 0.125, ((0, 4),)),
        "rate_weight": centred(streams_of[4], (SECTIONS, D, HW), D ** -0.5, 0.125, ((0, 4),)),
        "rate_bias": jnp.clip(jax.random.uniform(streams_of[5], (SECTIONS, HW), jnp.float32, -1.0, 1.0) * level_of(streams_of[5], (SECTIONS, HW), ((0, 4),), -0.4, 0.0), -1.0, 1.0),
        "decay_rate": jnp.clip(jnp.exp(math.log(0.03) - 5.5043554 * jax.random.uniform(streams_of[6], (SECTIONS, HW), jnp.float32) ** level_of(streams_of[6], (SECTIONS, HW), ((0, 4),), -0.2, 0.2)), 0.00012207031, 0.03),
        "level_table": jnp.clip(jnp.exp(math.log(2.0) - 2.0794415 * jax.random.uniform(streams_of[7], (SECTIONS, BUCKETS, LEVELS, HW), jnp.float32) ** level_of(streams_of[7], (SECTIONS, BUCKETS, LEVELS, HW), ((0, 4),), -0.2, 0.2)), 0.25, 2.0),
        "level_ids": with_ends(jax.random.randint(streams_of[8], (SECTIONS, TOKENS, LEVELS), 0, BUCKETS), jax.random.fold_in(streams_of[8], 1), 0, BUCKETS - 1).astype(jnp.int32),
        "out_gain": jnp.clip(1.0 + 0.1 * jax.random.normal(streams_of[9], (SECTIONS, HW * P_SIZE), jnp.float32), 0.5, 1.5),
        "out_weight": centred(streams_of[10], (SECTIONS, HW * P_SIZE, D), (HW * P_SIZE) ** -0.5, 0.1875, ((0, 4),)),
    }


EPSILON = 1e-05

def bit_table(rows_here, bits_tok):
    position = jnp.arange(rows_here, dtype=jnp.int32)
    flipped = position[:, None] ^ position[None, :]
    bit_level = jnp.zeros((rows_here, rows_here), jnp.int32)
    for bit_pos in range(bits_tok):
        bit_level = bit_level + (flipped >= 1 << bit_pos).astype(jnp.int32)
    return (bit_level, position[:, None] >= position[None, :])

def nearby_block(queries, key_rows, values, running, level_weight):
    bit_level, causal = bit_table(TOK_DEV, TOK_BITS)
    scores = jnp.dot(queries, key_rows.T, preferred_element_type=jnp.float32)
    by_head = running.T
    exponent = jnp.where(causal[None], by_head[:, :, None] - by_head[:, None, :], -jnp.inf)
    weight_heads = jnp.transpose(level_weight, (2, 0, 1))
    weight = jnp.zeros(exponent.shape, jnp.float32)
    for degree in range(TOK_BITS + 1):
        weight = weight + jnp.where(bit_level[None] == degree, weight_heads[:, :, degree:degree + 1], 0.0)
    mixing = (weight * jnp.exp(exponent) * scores[None]).astype(jnp.bfloat16)
    return jnp.einsum('htu,uhp->thp', mixing.astype(jnp.float32), values.astype(jnp.float32), precision=lax.Precision.HIGHEST)

def apply_layer(stream, norm_gain, value_weight, shared_weight, rate_weight, rate_bias, decay_rate, level_table, level_ids, out_gain, out_weight):
    widened = stream.astype(jnp.float32)
    normed = (widened * lax.rsqrt(lax.optimization_barrier(jnp.mean(widened * widened, axis=-1, keepdims=True)) + EPSILON) * norm_gain).astype(jnp.bfloat16)
    values_raw = jnp.dot(normed, value_weight, preferred_element_type=jnp.float32)
    shared_raw = jnp.dot(normed, shared_weight, preferred_element_type=jnp.float32)
    rates_raw = jnp.dot(normed, rate_weight, preferred_element_type=jnp.float32)
    step_size = jax.nn.softplus(rates_raw + rate_bias)
    log_decay = -decay_rate * step_size
    running = jnp.cumsum(log_decay.reshape(N_SEQ, TOK_DEV, HW), axis=1)
    block_decay = running[:, -1, :]
    starts = jnp.cumsum(block_decay, axis=0) - block_decay
    values = (values_raw.reshape(TOKENS, HW, P_SIZE) * step_size[:, :, None]).astype(jnp.bfloat16).reshape(N_SEQ, TOK_DEV, HW, P_SIZE)
    key_rows = shared_raw[:, :N].astype(jnp.bfloat16).reshape(N_SEQ, TOK_DEV, N)
    queries = shared_raw[:, N:].astype(jnp.bfloat16).reshape(N_SEQ, TOK_DEV, N)
    level_weight = level_table[level_ids, jnp.arange(LEVELS, dtype=jnp.int32)[None, :]].reshape(N_SEQ, TOK_DEV, LEVELS, HW)
    decayed = (values.astype(jnp.float32) * jnp.exp(block_decay[:, None, :] - running)[..., None]).astype(jnp.bfloat16)
    states = jnp.einsum('jun,juhp->jhnp', key_rows.astype(jnp.float32), decayed.astype(jnp.float32), precision=lax.Precision.HIGHEST)
    nearby = lax.map(lambda item: nearby_block(*item), (queries, key_rows, values, running, level_weight))
    block_ids = jnp.arange(N_SEQ, dtype=jnp.int32)
    ends = starts + block_decay

    def distant_block(item):
        block_index, query_blk, running_blk, weight_blk, start_blk = item
        found = []
        for degree in range(SEQ_BITS):
            member = (block_ids >> degree + 1 == block_index >> degree + 1) & (block_ids >> degree & 1 == 0) & (block_index >> degree & 1 == 1)
            exponent = jnp.where(member[:, None], start_blk[None, :] - ends, 0.0)
            factor = jnp.where(member[:, None], jnp.exp(exponent), 0.0)
            found.append(jnp.einsum('jh,jhnp->hnp', factor, states, precision=lax.Precision.HIGHEST))
        stacked = jnp.stack(found, axis=1).reshape(HW, SEQ_BITS * N, P_SIZE)
        query_coef = weight_blk[:, TOK_BITS + 1:, :] * jnp.exp(running_blk)[:, None, :]
        scaled = (query_blk.astype(jnp.float32)[:, None, None, :] * jnp.transpose(query_coef, (0, 2, 1))[:, :, :, None]).reshape(TOK_DEV, HW, SEQ_BITS * N)
        return jnp.einsum('thk,hkp->thp', scaled, stacked, precision=lax.Precision.HIGHEST)
    distant = lax.map(distant_block, (block_ids, queries, running, level_weight, starts))
    mixed = (nearby + distant).reshape(TOKENS, HW * P_SIZE)
    normed_mix = (mixed * lax.rsqrt(lax.optimization_barrier(jnp.mean(mixed * mixed, axis=-1, keepdims=True)) + EPSILON) * out_gain).astype(jnp.bfloat16)
    return (widened + jnp.dot(normed_mix, out_weight, preferred_element_type=jnp.float32)).astype(jnp.bfloat16)

def reference(activations, norm_gain, value_weight, shared_weight, rate_weight, rate_bias, decay_rate, level_table, level_ids, out_gain, out_weight):
    params = (norm_gain, value_weight, shared_weight, rate_weight, rate_bias, decay_rate, level_table, level_ids, out_gain, out_weight)
    handed = lax.map(lambda item: apply_layer(item[0], *item[1:]), (activations,) + params)
    arrived = jnp.roll(handed, 1, axis=0)
    return lax.map(lambda item: apply_layer(item[0], *item[1:]), (arrived,) + params)
```

```python
import functools

import jax
import jax.numpy as jnp
from jax import lax
from jax.experimental import pallas as pl
from jax.experimental.pallas import tpu as pltpu
from jax.sharding import PartitionSpec as P

EPSILON = 1e-05
CHUNK = 128
SLOT = 16
F32 = jnp.float32
BF16 = jnp.bfloat16


def dot(a, b):
    return jnp.dot(a, b, preferred_element_type=F32)


def dot_nt(a, b):
    return lax.dot_general(a, b, (((1,), (1,)), ((), ())), preferred_element_type=F32)


def dot_tn(a, b):
    return lax.dot_general(a, b, (((0,), (0,)), ((), ())), preferred_element_type=F32)


def iota(shape, dim):
    return lax.broadcasted_iota(jnp.int32, shape, dim)


def split3(x):
    hi = x.astype(BF16)
    rest = x - hi.astype(F32)
    mid = rest.astype(BF16)
    return hi, mid, (rest - mid.astype(F32)).astype(BF16)


def spread(row, heads, width):
    rows = row.shape[0]
    return jnp.concatenate(
        [
            jnp.broadcast_to(row[:, h * SLOT : h * SLOT + 1], (rows, width))
            for h in range(heads)
        ],
        axis=1,
    )


def weights_kernel(ids_ref, table_ref, lw_ref):
    lanes = table_ref.shape[0]
    pick = (iota((ids_ref.shape[1], lanes), 0) == iota((ids_ref.shape[1], lanes), 1) // SLOT)
    ids = dot(ids_ref[...], pick.astype(BF16))
    onehot = (ids == (iota(ids.shape, 1) % SLOT).astype(F32)).astype(BF16)
    hi, mid, lo = split3(table_ref[...])
    lw_ref[...] = dot(onehot, hi) + dot(onehot, mid) + dot(onehot, lo)


def tick_kernel(
    heads,
    bits,
    tok_bits,
    x_ref,
    gain_ref,
    wv_ref,
    ws_ref,
    wr_ref,
    bias_ref,
    rate_ref,
    lw_ref,
    out_gain_ref,
    wo_ref,
    y_ref,
    normed,
    step,
    local,
    vals,
    qk,
    acc,
    nmix,
    parts,
    inner,
    subtree,
    send,
    recv,
    send_sem,
    recv_sem,
):
    rows, width = x_ref.shape
    inner_width = heads * CHUNK
    n = CHUNK
    chunks = rows // CHUNK
    inner_bits = chunks.bit_length() - 1
    base = tok_bits - inner_bits
    me = lax.axis_index("seq")

    def bit_of(d):
        return (me // (1 << d)) % 2

    def partner_of(d):
        return me + (1 << d) * (1 - 2 * bit_of(d))

    barrier = pltpu.get_barrier_semaphore()
    for d in range(bits):
        pl.semaphore_signal(barrier, inc=1, device_id={"seq": partner_of(d)}, device_id_type=pl.DeviceIdType.MESH)
    pl.semaphore_wait(barrier, bits)

    @pl.loop(0, chunks)
    def _(c):
        at = pl.ds(pl.multiple_of(c * CHUNK, CHUNK), CHUNK)
        x = x_ref[at, :].astype(F32)
        scale = lax.rsqrt(jnp.mean(x * x, axis=-1, keepdims=True) + EPSILON)
        normed[at, :] = (x * scale * gain_ref[...]).astype(BF16)

    u = dot(normed[...], wr_ref[...]) + bias_ref[...]
    step[...] = jnp.maximum(u, 0.0) + jnp.log1p(jnp.exp(-jnp.abs(u)))
    tri = (iota((CHUNK, CHUNK), 0) >= iota((CHUNK, CHUNK), 1)).astype(BF16)

    totals = []
    for c in range(chunks):
        at = slice(c * CHUNK, (c + 1) * CHUNK)
        hi, mid, lo = split3(-rate_ref[...] * step[at, :])
        cs = dot(tri, hi) + dot(tri, mid) + dot(tri, lo)
        local[at, :] = cs
        totals.append(cs[CHUNK - 1 :, :])

    qk[...] = dot(normed[...], ws_ref[...]).astype(BF16)
    pair = 2 * CHUNK
    for c in range(inner_width // pair):
        raw = dot(normed[...], wv_ref[:, c * pair : (c + 1) * pair])
        for h in (2 * c, 2 * c + 1):
            col = slice((h - 2 * c) * CHUNK, (h - 2 * c + 1) * CHUNK)
            vals[:, h * CHUNK : (h + 1) * CHUNK] = (
                raw[:, col] * step[:, h * SLOT : h * SLOT + 1]
            ).astype(BF16)

    for c in range(chunks):
        at = slice(c * CHUNK, (c + 1) * CHUNK)
        fade = jnp.exp(totals[c] - local[at, :])
        decayed = (vals[at, :].astype(F32) * spread(fade, heads, CHUNK)).astype(BF16)
        parts[at, :] = dot_tn(qk[at, :n], decayed)

    group = {c: (parts[c * CHUNK : (c + 1) * CHUNK, :], totals[c]) for c in range(chunks)}
    slots = []
    for e in range(inner_bits):
        merged = {}
        for g in range(0, len(group), 2):
            (low, low_total), (high, high_total) = group[g], group[g + 1]
            inner[len(slots) * n : (len(slots) + 1) * n, :] = low.astype(BF16)
            slots.append((e, g + 1))
            merged[g // 2] = (
                low * jnp.exp(spread(high_total, heads, CHUNK)) + high,
                low_total + high_total,
            )
        group = merged
    own, total = group[0]
    subtree[...] = own
    total = spread(total, heads, CHUNK)

    def put(d, decay):
        send[d, :n, :] = subtree[...].astype(BF16)
        hi, mid, lo = split3(decay)
        row = iota((SLOT, inner_width), 0)
        tail = jnp.where(row == 0, hi.astype(F32), jnp.where(row == 1, mid.astype(F32), jnp.where(row == 2, lo.astype(F32), 0.0)))
        send[d, n:, :] = tail.astype(BF16)
        copy = pltpu.make_async_remote_copy(
            src_ref=send.at[d],
            dst_ref=recv.at[d],
            send_sem=send_sem.at[d],
            recv_sem=recv_sem.at[d],
            device_id={"seq": partner_of(d)},
            device_id_type=pl.DeviceIdType.MESH,
        )
        copy.start()
        return copy

    position_t = iota((CHUNK, CHUNK), 0)
    position_u = iota((CHUNK, CHUNK), 1)
    causal = position_t >= position_u
    flipped = position_t ^ position_u
    level = jnp.zeros((CHUNK, CHUNK), jnp.int32)
    for b in range(base):
        level = level + (flipped >= (1 << b)).astype(jnp.int32)

    def near(c):
        at = slice(c * CHUNK, (c + 1) * CHUNK)
        scores = jnp.where(causal, dot_nt(qk[at, n:], qk[at, :n]), 0.0)
        run = local[at, :]
        run_t = run.T
        weights = lw_ref[at, :]
        for h in range(heads):
            lane = h * SLOT
            exponent = run[:, lane : lane + 1] - run_t[lane : lane + 1, :]
            weight = jnp.take_along_axis(weights, level + lane, axis=1)
            mixing = (weight * jnp.exp(jnp.minimum(exponent, 0.0)) * scores).astype(BF16)
            col = slice(h * CHUNK, (h + 1) * CHUNK)
            acc[at, col] = dot(mixing, vals[at, col])

    def near_states(c):
        at = slice(c * CHUNK, (c + 1) * CHUNK)
        for slot, (e, g) in enumerate(slots):
            if c >> e != g:
                continue
            prefix = sum([totals[m] for m in range(g << e, c)], jnp.zeros_like(totals[0]))
            coef = lw_ref[at, :] * jnp.exp(local[at, :] + prefix)
            add_level(at, coef, base + e + 1, inner[slot * n : (slot + 1) * n, :])

    def add_level(at, coef, l, state):
        far = dot(qk[at, n:], state)
        for h in range(heads):
            col = slice(h * CHUNK, (h + 1) * CHUNK)
            acc[at, col] += coef[:, h * SLOT + l : h * SLOT + l + 1] * far[:, col]

    def distant(d, prefix):
        upper = bit_of(d) == 1
        factor = jnp.where(upper, jnp.exp(prefix), 0.0)
        state = (recv[d, :n, :].astype(F32) * factor).astype(BF16)
        for c in range(chunks):
            at = slice(c * CHUNK, (c + 1) * CHUNK)
            before = sum(totals[:c], jnp.zeros_like(totals[0]))
            coef = lw_ref[at, :] * jnp.exp(local[at, :] + before)
            add_level(at, coef, tok_bits + 1 + d, state)

    decay = total
    prefix = jnp.zeros_like(total)
    prefixes = []
    work = [functools.partial(near, c) for c in range(chunks)]
    share = -(-len(work) // 2)
    copy = put(0, decay)
    for d in range(bits):
        if d < 2:
            for item in work[d * share : (d + 1) * share]:
                item()
        if d == 1 or bits == 1:
            pass
        if d == 2 or bits < 3 and d == bits - 1:
            for c in range(chunks):
                near_states(c)
        if d >= 2:
            distant(d - 2, prefixes[d - 2])
        copy.wait()
        tail = recv[d, n:, :].astype(F32)
        partner_decay = tail[0:1, :] + tail[1:2, :] + tail[2:3, :]
        prefixes.append(prefix)
        upper = bit_of(d) == 1
        if d < bits - 1:
            mine = jnp.exp(jnp.where(upper, 0.0, partner_decay))
            theirs = jnp.exp(jnp.where(upper, decay, 0.0))
            subtree[...] = subtree[...] * mine + recv[d, :n, :].astype(F32) * theirs
            prefix = jnp.where(upper, prefix + partner_decay, prefix)
            decay = decay + partner_decay
            copy = put(d + 1, decay)
    for d in range(max(bits - 2, 0), bits):
        distant(d, prefixes[d])

    for c in range(chunks):
        at = slice(c * CHUNK, (c + 1) * CHUNK)
        mixed = acc[at, :]
        scale = lax.rsqrt(jnp.mean(mixed * mixed, axis=-1, keepdims=True) + EPSILON)
        nmix[at, :] = (mixed * scale * out_gain_ref[...]).astype(BF16)

    @pl.loop(0, width // pair)
    def _(c):
        at = pl.ds(pl.multiple_of(c * pair, pair), pair)
        y_ref[:, at] = (x_ref[:, at].astype(F32) + dot(nmix[...], wo_ref[:, at])).astype(BF16)


def passed_along(block, axis, distance):
    devices = range(lax.axis_size(axis))
    route = [((i - distance) % len(devices), i) for i in devices]
    return lax.ppermute(block, axis, route)


def vmem(count):
    return [pl.BlockSpec(memory_space=pltpu.VMEM)] * count


def body(
    activations,
    norm_gain,
    value_weight,
    shared_weight,
    rate_weight,
    rate_bias,
    decay_rate,
    level_table,
    level_ids,
    out_gain,
    out_weight,
):
    rows, width = activations.shape[1:]
    heads = rate_bias.shape[1]
    buckets, levels = level_table.shape[1:3]
    inner_width = value_weight.shape[2]
    tok_bits = rows.bit_length() - 1
    bits = lax.axis_size("seq").bit_length() - 1
    chunks = rows // CHUNK
    table = jnp.transpose(level_table[0], (1, 0, 2))
    table = jnp.pad(table, ((0, SLOT - levels), (0, SLOT - buckets), (0, 0)))
    spot = jnp.arange(SLOT)
    table = jnp.where(
        spot[:, None, None, None] == spot[None, None, None, :], table[:, :, :, None], 0.0
    ).reshape(SLOT * SLOT, heads * SLOT)
    ids = jnp.pad(level_ids[0].astype(BF16), ((0, 0), (0, CHUNK - levels)))
    lw = pl.pallas_call(
        weights_kernel,
        out_shape=jax.ShapeDtypeStruct((rows, heads * SLOT), F32),
        in_specs=vmem(2),
        out_specs=vmem(1)[0],
    )(ids, table)
    tick = pl.pallas_call(
        functools.partial(tick_kernel, heads, bits, tok_bits),
        out_shape=jax.ShapeDtypeStruct((rows, width), BF16),
        in_specs=vmem(10),
        out_specs=vmem(1)[0],
        scratch_shapes=[
            pltpu.VMEM((rows, width), BF16),
            pltpu.VMEM((rows, heads * SLOT), F32),
            pltpu.VMEM((rows, heads * SLOT), F32),
            pltpu.VMEM((rows, inner_width), BF16),
            pltpu.VMEM((rows, shared_weight.shape[2]), BF16),
            pltpu.VMEM((rows, inner_width), F32),
            pltpu.VMEM((rows, inner_width), BF16),
            pltpu.VMEM((rows, inner_width), F32),
            pltpu.VMEM((max(chunks - 1, 1) * CHUNK, inner_width), BF16),
            pltpu.VMEM((CHUNK, inner_width), F32),
            pltpu.VMEM((bits, CHUNK + SLOT, inner_width), BF16),
            pltpu.VMEM((bits, CHUNK + SLOT, inner_width), BF16),
            pltpu.SemaphoreType.DMA((bits,)),
            pltpu.SemaphoreType.DMA((bits,)),
        ],
        compiler_params=pltpu.CompilerParams(
            collective_id=0, has_side_effects=True, vmem_limit_bytes=56 * 1024 * 1024
        ),
    )
    rate_wide = jnp.repeat(rate_weight[0], SLOT, axis=1)
    bias_wide = jnp.repeat(rate_bias, SLOT, axis=1)
    decay_wide = jnp.repeat(decay_rate, SLOT, axis=1)

    def layer(stream):
        return tick(
            stream,
            norm_gain,
            value_weight[0],
            shared_weight[0],
            rate_wide,
            bias_wide,
            decay_wide,
            lw,
            out_gain,
            out_weight[0],
        )

    handed = layer(activations[0])
    return layer(passed_along(handed, "section", 1))[None]


def solution(mesh):
    placed = (
        P("section", "seq", None),
        P("section", None),
        P("section", None, None),
        P("section", None, None),
        P("section", None, None),
        P("section", None),
        P("section", None),
        P("section", None, None, None),
        P("section", "seq", None),
        P("section", None),
        P("section", None, None),
    )
    return jax.shard_map(
        body, mesh=mesh, in_specs=placed, out_specs=P("section", "seq", None), check_vma=False
    )
```

```python
import functools

import jax
import jax.numpy as jnp
from jax import lax
from jax.experimental import pallas as pl
from jax.experimental.pallas import tpu as pltpu
from jax.sharding import PartitionSpec as P

EPSILON = 1e-05
CHUNK = 128
SLOT = 16
F32 = jnp.float32
BF16 = jnp.bfloat16


def dot(a, b):
    return jnp.dot(a, b, preferred_element_type=F32)


def dot_nt(a, b):
    return lax.dot_general(a, b, (((1,), (1,)), ((), ())), preferred_element_type=F32)


def dot_tn(a, b):
    return lax.dot_general(a, b, (((0,), (0,)), ((), ())), preferred_element_type=F32)


def iota(shape, dim):
    return lax.broadcasted_iota(jnp.int32, shape, dim)


def split3(x):
    hi = x.astype(BF16)
    rest = x - hi.astype(F32)
    mid = rest.astype(BF16)
    return hi, mid, (rest - mid.astype(F32)).astype(BF16)


def spread(row, heads, width):
    rows = row.shape[0]
    return jnp.concatenate(
        [
            jnp.broadcast_to(row[:, h * SLOT : h * SLOT + 1], (rows, width))
            for h in range(heads)
        ],
        axis=1,
    )


def widen(v, heads):
    expand = (iota((heads, heads * SLOT), 0) == iota((heads, heads * SLOT), 1) // SLOT).astype(BF16)
    return sum(dot(part, expand) for part in split3(v))


def ticks_kernel(
    heads,
    bits,
    tok_bits,
    pieces,
    x_ref,
    gain_ref,
    wv_hbm,
    ws_hbm,
    wr_ref,
    bias_ref,
    rate_ref,
    table_ref,
    ids_ref,
    out_gain_ref,
    wo_hbm,
    nmix,
    arrived_hbm,
    wv_ref,
    ws_ref,
    wo_ref,
    lw_ref,
    normed,
    step,
    local,
    vals,
    qk,
    acc,
    parts,
    inner,
    subtree,
    totals_ref,
    handed,
    arrived,
    send,
    recv,
    load_sem,
    send_sem,
    recv_sem,
    hand_send_sem,
    hand_recv_sem,
):
    rows, width = x_ref.shape
    inner_width = heads * CHUNK
    n = CHUNK
    chunks = rows // CHUNK
    inner_bits = chunks.bit_length() - 1
    base = tok_bits - inner_bits
    pair = inner_width // pieces
    pair_heads = heads // pieces
    me = lax.axis_index("seq")
    sections = lax.axis_size("section")
    section = lax.axis_index("section")
    following = (section + 1) % sections
    previous = (section + sections - 1) % sections
    mesh_ids = pl.DeviceIdType.MESH

    def bit_of(d):
        return (me // (1 << d)) % 2

    def partner_of(d):
        return me + (1 << d) * (1 - 2 * bit_of(d))

    loads = [
        pltpu.make_async_copy(src, dst, load_sem.at[i])
        for i, (src, dst) in enumerate(((ws_hbm, ws_ref), (wv_hbm, wv_ref), (wo_hbm, wo_ref)))
    ]
    for load in loads:
        load.start()
    barrier = pltpu.get_barrier_semaphore()
    for d in range(bits):
        pl.semaphore_signal(barrier, inc=1, device_id={"seq": partner_of(d)}, device_id_type=mesh_ids)
    for other in (following, previous):
        pl.semaphore_signal(barrier, inc=1, device_id={"section": other}, device_id_type=mesh_ids)
    pl.semaphore_wait(barrier, bits + 2)

    lanes = table_ref.shape[0]
    spot = (lanes, heads * SLOT)
    table = jnp.where(
        iota(spot, 0) // SLOT == iota(spot, 1) % SLOT, widen(table_ref[...], heads), 0.0
    )
    pick = iota((CHUNK, lanes), 0) == iota((CHUNK, lanes), 1) // SLOT
    ids = dot(ids_ref[...], pick.astype(BF16))
    onehot = (ids == (iota(ids.shape, 1) % SLOT).astype(F32)).astype(BF16)
    lw_ref[...] = sum(dot(onehot, part) for part in split3(table))
    rate_wide = dot(wr_ref[...], (iota((heads, heads * SLOT), 0) == iota((heads, heads * SLOT), 1) // SLOT).astype(BF16)).astype(BF16)
    bias = widen(jnp.broadcast_to(bias_ref[...], (8, heads)), heads)[:1, :]
    rate = widen(jnp.broadcast_to(rate_ref[...], (8, heads)), heads)[:1, :]
    tri = (iota((CHUNK, CHUNK), 0) >= iota((CHUNK, CHUNK), 1)).astype(BF16)

    position_t = iota((CHUNK, CHUNK), 0)
    position_u = iota((CHUNK, CHUNK), 1)
    causal = position_t >= position_u
    flipped = position_t ^ position_u
    level = jnp.zeros((CHUNK, CHUNK), jnp.int32)
    for b in range(base):
        level = level + (flipped >= (1 << b)).astype(jnp.int32)

    def handoff(c):
        at = pl.ds(pl.multiple_of(c * CHUNK, CHUNK), CHUNK)
        return pltpu.make_async_remote_copy(
            src_ref=handed.at[at, :],
            dst_ref=arrived.at[at, :],
            send_sem=hand_send_sem.at[c],
            recv_sem=hand_recv_sem.at[c],
            device_id={"section": following},
            device_id_type=mesh_ids,
        )

    def exchange(t, d, p):
        return pltpu.make_async_remote_copy(
            src_ref=send.at[t, d, p],
            dst_ref=recv.at[t, d, p],
            send_sem=send_sem.at[t, d, p],
            recv_sem=recv_sem.at[t, d, p],
            device_id={"seq": partner_of(d)},
            device_id_type=mesh_ids,
        )

    def project(first, size, source, t):
        group = pl.ds(pl.multiple_of(first * CHUNK, CHUNK), size)

        @pl.loop(0, size // CHUNK)
        def _(i):
            at = pl.ds(pl.multiple_of((first + i) * CHUNK, CHUNK), CHUNK)
            x = source[at, :].astype(F32)
            scale = lax.rsqrt(jnp.mean(x * x, axis=-1, keepdims=True) + EPSILON)
            normed[at, :] = (x * scale * gain_ref[...]).astype(BF16)

        u = dot(normed[group, :], rate_wide) + bias
        step[group, :] = jnp.maximum(u, 0.0) + jnp.log1p(jnp.exp(-jnp.abs(u)))
        if t == 0:
            loads[0].wait()
        qk[group, :] = dot(normed[group, :], ws_ref[...]).astype(BF16)
        if t == 0:
            loads[1].wait()
        for p in range(pieces):
            raw = dot(normed[group, :], wv_ref[:, p * pair : (p + 1) * pair])
            for i in range(pair_heads):
                h = p * pair_heads + i
                vals[group, h * CHUNK : (h + 1) * CHUNK] = (
                    raw[:, i * CHUNK : (i + 1) * CHUNK] * step[group, h * SLOT : h * SLOT + 1]
                ).astype(BF16)

        @pl.loop(0, size // CHUNK)
        def _(i):
            c = first + i
            at = pl.ds(pl.multiple_of(c * CHUNK, CHUNK), CHUNK)
            cs = sum(dot(tri, part) for part in split3(-rate * step[at, :]))
            local[at, :] = cs
            whole = cs[CHUNK - 1 :, :]
            totals_ref[c] = jnp.broadcast_to(whole, (8, heads * SLOT))
            fade = jnp.exp(whole - cs)
            decayed = (vals[at, :].astype(F32) * spread(fade, heads, CHUNK)).astype(BF16)
            parts[at, :] = dot_tn(qk[at, :n], decayed)

    def tick(t):
        if t == 0:
            project(0, rows, x_ref, t)
        else:

            @pl.loop(0, chunks)
            def _(c):
                handoff(c).wait_recv()
                project(c, CHUNK, arrived, t)

        totals = [totals_ref[c][:1, :] for c in range(chunks)]
        group_totals = {}
        for e in range(inner_bits + 1):
            for g in range(chunks >> e):
                group_totals[e, g] = sum(totals[(g << e) + 1 : (g + 1) << e], totals[g << e])
        slots = [(e, g) for e in range(inner_bits) for g in range(1, chunks >> e, 2)]
        wide = {
            key: spread(value, heads, CHUNK)
            for key, value in group_totals.items()
        }

        def put(d, p, decay):
            cols = slice(p * pair, (p + 1) * pair)
            send[t, d, p, :n, :] = subtree[:, cols].astype(BF16)
            row = iota((SLOT, pair), 0)
            tail = jnp.zeros((SLOT, pair), F32)
            for i, part in enumerate(split3(decay)):
                tail = jnp.where(row == i, part.astype(F32), tail)
            send[t, d, p, n:, :] = tail.astype(BF16)
            exchange(t, d, p).start()

        decay = wide[inner_bits, 0]
        for p in range(pieces):
            cols = slice(p * pair, (p + 1) * pair)
            group = [parts[c * CHUNK : (c + 1) * CHUNK, cols] for c in range(chunks)]
            slot = 0
            for e in range(inner_bits):
                merged = []
                for g in range(0, len(group), 2):
                    inner[slot * n : (slot + 1) * n, cols] = group[g].astype(BF16)
                    slot += 1
                    merged.append(
                        group[g] * jnp.exp(wide[e, g + 1][:, cols]) + group[g + 1]
                    )
                group = merged
            subtree[:, cols] = group[0]
            put(0, p, decay[:, cols])

        def near(c):
            at = slice(c * CHUNK, (c + 1) * CHUNK)
            scores = jnp.where(causal, dot_nt(qk[at, n:], qk[at, :n]), 0.0)
            run = local[at, :]
            run_t = run.T
            weights = lw_ref[at, :]
            for h in range(heads):
                lane = h * SLOT
                exponent = run[:, lane : lane + 1] - run_t[lane : lane + 1, :]
                weight = jnp.take_along_axis(weights, level + lane, axis=1)
                mixing = (weight * jnp.exp(jnp.minimum(exponent, 0.0)) * scores).astype(BF16)
                col = slice(h * CHUNK, (h + 1) * CHUNK)
                acc[at, col] = dot(mixing, vals[at, col])

        def add_level(at, coef, l, state):
            far = dot(qk[at, n:], state)
            for h in range(heads):
                col = slice(h * CHUNK, (h + 1) * CHUNK)
                acc[at, col] += coef[:, h * SLOT + l : h * SLOT + l + 1] * far[:, col]

        def near_states(c):
            at = slice(c * CHUNK, (c + 1) * CHUNK)
            for slot, (e, g) in enumerate(slots):
                if c >> e != g:
                    continue
                prefix = sum(totals[g << e : c], jnp.zeros_like(totals[0]))
                coef = lw_ref[at, :] * jnp.exp(local[at, :] + prefix)
                add_level(at, coef, base + e + 1, inner[slot * n : (slot + 1) * n, :])

        def far_state(d, prefix):
            factor = jnp.where(bit_of(d) == 1, jnp.exp(prefix), 0.0)
            return jnp.concatenate(
                [
                    (recv[t, d, p, :n, :].astype(F32) * factor[:, p * pair : (p + 1) * pair]).astype(BF16)
                    for p in range(pieces)
                ],
                axis=1,
            )

        def distant(c, d, state):
            at = slice(c * CHUNK, (c + 1) * CHUNK)
            before = sum(totals[:c], jnp.zeros_like(totals[0]))
            coef = lw_ref[at, :] * jnp.exp(local[at, :] + before)
            add_level(at, coef, tok_bits + 1 + d, state)

        work = [functools.partial(near, c) for c in range(chunks)]
        work += [functools.partial(near_states, c) for c in range(1, chunks)]
        prefix = jnp.zeros_like(decay)
        prefixes = []
        taken = 0
        for d in range(bits):
            stop = len(work) * (2 * d + 2) // (2 * bits) if d < bits - 1 else len(work)
            for item in work[taken:stop]:
                item()
            taken = stop
            if d >= 2:
                for e in range(d - 2, d) if d == bits - 1 else (d - 2,):
                    state = far_state(e, prefixes[e])
                    for c in range(chunks):
                        distant(c, e, state)
            upper = bit_of(d) == 1
            prefixes.append(prefix)
            found = []
            for p in range(pieces):
                cols = slice(p * pair, (p + 1) * pair)
                exchange(t, d, p).wait()
                if d == bits - 1:
                    continue
                tail = recv[t, d, p, n:, :].astype(F32)
                there = tail[0:1, :] + tail[1:2, :] + tail[2:3, :]
                here = decay[:, cols]
                mine = jnp.exp(jnp.where(upper, 0.0, there))
                theirs = jnp.exp(jnp.where(upper, here, 0.0))
                subtree[:, cols] = subtree[:, cols] * mine + recv[t, d, p, :n, :].astype(F32) * theirs
                found.append(there)
                put(d + 1, p, here + there)
            if d < bits - 1:
                there = jnp.concatenate(found, axis=1)
                prefix = jnp.where(upper, prefix + there, prefix)
                decay = decay + there
        rest = range(bits - 1, bits) if bits >= 3 else range(bits)
        states = [(d, far_state(d, prefixes[d])) for d in rest]
        if t == 0:
            loads[2].wait()
        for c in range(chunks):
            at = slice(c * CHUNK, (c + 1) * CHUNK)
            for d, state in states:
                distant(c, d, state)
            mixed = acc[at, :]
            scale = lax.rsqrt(jnp.mean(mixed * mixed, axis=-1, keepdims=True) + EPSILON)
            nmix[at, :] = (mixed * scale * out_gain_ref[...]).astype(BF16)
            if t == 0:

                @pl.loop(0, width // (2 * CHUNK))
                def _(i):
                    col = pl.ds(pl.multiple_of(i * 2 * CHUNK, 2 * CHUNK), 2 * CHUNK)
                    handed[at, col] = (
                        x_ref[at, col].astype(F32) + dot(nmix[at, :], wo_ref[:, col])
                    ).astype(BF16)

                handoff(c).start()

    tick(0)
    tick(1)
    keep = pltpu.make_async_copy(arrived, arrived_hbm, load_sem.at[0])
    keep.start()
    for c in range(chunks):
        handoff(c).wait_send()
    keep.wait()


def body(
    activations,
    norm_gain,
    value_weight,
    shared_weight,
    rate_weight,
    rate_bias,
    decay_rate,
    level_table,
    level_ids,
    out_gain,
    out_weight,
):
    rows, width = activations.shape[1:]
    heads = rate_bias.shape[1]
    buckets, levels = level_table.shape[1:3]
    inner_width = value_weight.shape[2]
    tok_bits = rows.bit_length() - 1
    bits = lax.axis_size("seq").bit_length() - 1
    chunks = rows // CHUNK
    pieces = heads // 2
    table = jnp.transpose(level_table[0], (1, 0, 2))
    table = jnp.pad(table, ((0, SLOT - levels), (0, SLOT - buckets), (0, 0)))
    table = table.reshape(SLOT * SLOT, heads)
    ids = jnp.pad(level_ids[0].astype(BF16), ((0, 0), (0, CHUNK - levels)))
    hbm = pl.BlockSpec(memory_space=pl.ANY)
    near = pl.BlockSpec(memory_space=pltpu.VMEM)
    states = (2, bits, pieces, CHUNK + SLOT, inner_width // pieces)
    normed_mix, arrived = pl.pallas_call(
        functools.partial(ticks_kernel, heads, bits, tok_bits, pieces),
        out_shape=(
            jax.ShapeDtypeStruct((rows, inner_width), BF16),
            jax.ShapeDtypeStruct((rows, width), BF16),
        ),
        in_specs=[near, near, hbm, hbm, near, near, near, near, near, near, hbm],
        out_specs=(near, hbm),
        scratch_shapes=[
            pltpu.VMEM(value_weight.shape[1:], BF16),
            pltpu.VMEM(shared_weight.shape[1:], BF16),
            pltpu.VMEM(out_weight.shape[1:], BF16),
            pltpu.VMEM((rows, heads * SLOT), F32),
            pltpu.VMEM((rows, width), BF16),
            pltpu.VMEM((rows, heads * SLOT), F32),
            pltpu.VMEM((rows, heads * SLOT), F32),
            pltpu.VMEM((rows, inner_width), BF16),
            pltpu.VMEM((rows, shared_weight.shape[2]), BF16),
            pltpu.VMEM((rows, inner_width), F32),
            pltpu.VMEM((rows, inner_width), F32),
            pltpu.VMEM((max(chunks - 1, 1) * CHUNK, inner_width), BF16),
            pltpu.VMEM((CHUNK, inner_width), F32),
            pltpu.VMEM((chunks, 8, heads * SLOT), F32),
            pltpu.VMEM((rows, width), BF16),
            pltpu.VMEM((rows, width), BF16),
            pltpu.VMEM(states, BF16),
            pltpu.VMEM(states, BF16),
            pltpu.SemaphoreType.DMA((3,)),
            pltpu.SemaphoreType.DMA(states[:3]),
            pltpu.SemaphoreType.DMA(states[:3]),
            pltpu.SemaphoreType.DMA((chunks,)),
            pltpu.SemaphoreType.DMA((chunks,)),
        ],
        compiler_params=pltpu.CompilerParams(
            collective_id=0, has_side_effects=True, vmem_limit_bytes=56 * 1024 * 1024
        ),
    )(
        activations[0],
        norm_gain,
        value_weight[0],
        shared_weight[0],
        rate_weight[0],
        rate_bias,
        decay_rate,
        table,
        ids,
        out_gain,
        out_weight[0],
    )
    return (arrived.astype(F32) + dot(normed_mix, out_weight[0])).astype(BF16)[None]


def solution(mesh):
    placed = (
        P("section", "seq", None),
        P("section", None),
        P("section", None, None),
        P("section", None, None),
        P("section", None, None),
        P("section", None),
        P("section", None),
        P("section", None, None, None),
        P("section", "seq", None),
        P("section", None),
        P("section", None, None),
    )
    return jax.shard_map(
        body, mesh=mesh, in_specs=placed, out_specs=P("section", "seq", None), check_vma=False
    )
```

```python
import functools

import jax
import jax.numpy as jnp
from jax import lax
from jax.experimental import pallas as pl
from jax.experimental.pallas import tpu as pltpu
from jax.sharding import PartitionSpec as P

EPSILON = 1e-05
CHUNK = 128
SLOT = 16
F32 = jnp.float32
BF16 = jnp.bfloat16


def dot(a, b):
    return jnp.dot(a, b, preferred_element_type=F32)


def dot_nt(a, b):
    return lax.dot_general(a, b, (((1,), (1,)), ((), ())), preferred_element_type=F32)


def dot_tn(a, b):
    return lax.dot_general(a, b, (((0,), (0,)), ((), ())), preferred_element_type=F32)


def iota(shape, dim):
    return lax.broadcasted_iota(jnp.int32, shape, dim)


def split3(x):
    hi = x.astype(BF16)
    rest = x - hi.astype(F32)
    mid = rest.astype(BF16)
    return hi, mid, (rest - mid.astype(F32)).astype(BF16)


def spread(row, heads, width):
    rows = row.shape[0]
    return jnp.concatenate(
        [
            jnp.broadcast_to(row[:, h * SLOT : h * SLOT + 1], (rows, width))
            for h in range(heads)
        ],
        axis=1,
    )


def widen(v, heads):
    expand = (iota((heads, heads * SLOT), 0) == iota((heads, heads * SLOT), 1) // SLOT).astype(BF16)
    return sum(dot(part, expand) for part in split3(v))


def ticks_kernel(
    heads,
    bits,
    tok_bits,
    pieces,
    x_ref,
    gain_ref,
    wv_hbm,
    ws_hbm,
    wr_ref,
    bias_ref,
    rate_ref,
    table_ref,
    ids_ref,
    out_gain_ref,
    wo_hbm,
    nmix,
    arrived_hbm,
    wv_ref,
    ws_ref,
    wo_ref,
    lw_ref,
    normed,
    step,
    local,
    vals,
    qk,
    acc,
    parts,
    inner,
    subtree,
    totals_ref,
    handed,
    arrived,
    send,
    recv,
    load_sem,
    send_sem,
    recv_sem,
    hand_send_sem,
    hand_recv_sem,
):
    rows, width = x_ref.shape
    inner_width = heads * CHUNK
    n = CHUNK
    chunks = rows // CHUNK
    inner_bits = chunks.bit_length() - 1
    base = tok_bits - inner_bits
    pair = inner_width // pieces
    pair_heads = heads // pieces
    me = lax.axis_index("seq")
    sections = lax.axis_size("section")
    section = lax.axis_index("section")
    following = (section + 1) % sections
    previous = (section + sections - 1) % sections
    mesh_ids = pl.DeviceIdType.MESH

    def bit_of(d):
        return (me // (1 << d)) % 2

    def partner_of(d):
        return me + (1 << d) * (1 - 2 * bit_of(d))

    loads = [
        pltpu.make_async_copy(src, dst, load_sem.at[i])
        for i, (src, dst) in enumerate(((ws_hbm, ws_ref), (wv_hbm, wv_ref), (wo_hbm, wo_ref)))
    ]
    for load in loads:
        load.start()
    barrier = pltpu.get_barrier_semaphore()
    for d in range(bits):
        pl.semaphore_signal(barrier, inc=1, device_id={"seq": partner_of(d)}, device_id_type=mesh_ids)
    for other in (following, previous):
        pl.semaphore_signal(barrier, inc=1, device_id={"section": other}, device_id_type=mesh_ids)
    pl.semaphore_wait(barrier, bits + 2)

    lanes = table_ref.shape[0]
    spot = (lanes, heads * SLOT)
    table = jnp.where(
        iota(spot, 0) // SLOT == iota(spot, 1) % SLOT, widen(table_ref[...], heads), 0.0
    )
    levels = ids_ref.shape[0]
    pick = iota((levels, lanes), 0) == iota((levels, lanes), 1) // SLOT
    ids = dot_tn(ids_ref[...].astype(F32).astype(BF16), pick.astype(BF16))
    onehot = (ids == (iota(ids.shape, 1) % SLOT).astype(F32)).astype(BF16)
    lw_ref[...] = sum(dot(onehot, part) for part in split3(table))
    expand = iota((heads, heads * SLOT), 0) == iota((heads, heads * SLOT), 1) // SLOT
    rate_wide = dot_tn(expand.astype(BF16), wr_ref[...]).astype(BF16)
    bias = widen(jnp.broadcast_to(bias_ref[...], (8, heads)), heads)[:1, :]
    rate = widen(jnp.broadcast_to(rate_ref[...], (8, heads)), heads)[:1, :]
    tri = (iota((CHUNK, CHUNK), 0) >= iota((CHUNK, CHUNK), 1)).astype(BF16)

    position_t = iota((CHUNK, CHUNK), 0)
    position_u = iota((CHUNK, CHUNK), 1)
    causal = position_t >= position_u
    flipped = position_t ^ position_u
    level = jnp.zeros((CHUNK, CHUNK), jnp.int32)
    for b in range(base):
        level = level + (flipped >= (1 << b)).astype(jnp.int32)

    def handoff(c):
        at = pl.ds(pl.multiple_of(c * CHUNK, CHUNK), CHUNK)
        return pltpu.make_async_remote_copy(
            src_ref=handed.at[at, :],
            dst_ref=arrived.at[at, :],
            send_sem=hand_send_sem.at[c],
            recv_sem=hand_recv_sem.at[c],
            device_id={"section": following},
            device_id_type=mesh_ids,
        )

    def exchange(t, d, p):
        return pltpu.make_async_remote_copy(
            src_ref=send.at[t, d, p],
            dst_ref=recv.at[t, d, p],
            send_sem=send_sem.at[t, d, p],
            recv_sem=recv_sem.at[t, d, p],
            device_id={"seq": partner_of(d)},
            device_id_type=mesh_ids,
        )

    def project(first, size, source, t):
        group = pl.ds(pl.multiple_of(first * CHUNK, CHUNK), size)

        @pl.loop(0, size // CHUNK)
        def _(i):
            at = pl.ds(pl.multiple_of((first + i) * CHUNK, CHUNK), CHUNK)
            x = source[at, :].astype(F32)
            scale = lax.rsqrt(jnp.mean(x * x, axis=-1, keepdims=True) + EPSILON)
            normed[at, :] = (x * scale * gain_ref[...]).astype(BF16)

        u = dot_nt(normed[group, :], rate_wide) + bias
        step[group, :] = jnp.maximum(u, 0.0) + jnp.log1p(jnp.exp(-jnp.abs(u)))
        if t == 0:
            loads[0].wait()
        qk[group, :] = dot(normed[group, :], ws_ref[...]).astype(BF16)
        if t == 0:
            loads[1].wait()
        for p in range(pieces):
            raw = dot(normed[group, :], wv_ref[:, p * pair : (p + 1) * pair])
            for i in range(pair_heads):
                h = p * pair_heads + i
                vals[group, h * CHUNK : (h + 1) * CHUNK] = (
                    raw[:, i * CHUNK : (i + 1) * CHUNK] * step[group, h * SLOT : h * SLOT + 1]
                ).astype(BF16)

        @pl.loop(0, size // CHUNK)
        def _(i):
            c = first + i
            at = pl.ds(pl.multiple_of(c * CHUNK, CHUNK), CHUNK)
            cs = sum(dot(tri, part) for part in split3(-rate * step[at, :]))
            local[at, :] = cs
            whole = cs[CHUNK - 1 :, :]
            totals_ref[c] = jnp.broadcast_to(whole, (8, heads * SLOT))
            fade = jnp.exp(whole - cs)
            decayed = (vals[at, :].astype(F32) * spread(fade, heads, CHUNK)).astype(BF16)
            parts[at, :] = dot_tn(qk[at, :n], decayed)

    def tick(t):
        if t == 0:
            project(0, rows, x_ref, t)
        else:

            @pl.loop(0, chunks)
            def _(c):
                handoff(c).wait_recv()
                project(c, CHUNK, arrived, t)

        totals = [totals_ref[c][:1, :] for c in range(chunks)]
        group_totals = {}
        for e in range(inner_bits + 1):
            for g in range(chunks >> e):
                group_totals[e, g] = sum(totals[(g << e) + 1 : (g + 1) << e], totals[g << e])
        slots = [(e, g) for e in range(inner_bits) for g in range(1, chunks >> e, 2)]
        wide = {
            key: spread(value, heads, CHUNK)
            for key, value in group_totals.items()
        }

        def put(d, p, decay):
            cols = slice(p * pair, (p + 1) * pair)
            send[t, d, p, :n, :] = subtree[:, cols].astype(BF16)
            row = iota((SLOT, pair), 0)
            tail = jnp.zeros((SLOT, pair), F32)
            for i, part in enumerate(split3(decay)):
                tail = jnp.where(row == i, part.astype(F32), tail)
            send[t, d, p, n:, :] = tail.astype(BF16)
            exchange(t, d, p).start()

        def near(c):
            at = slice(c * CHUNK, (c + 1) * CHUNK)
            scores = jnp.where(causal, dot_nt(qk[at, n:], qk[at, :n]), 0.0)
            run = local[at, :]
            run_t = run.T
            weights = lw_ref[at, :]
            for h in range(heads):
                lane = h * SLOT
                exponent = run[:, lane : lane + 1] - run_t[lane : lane + 1, :]
                weight = jnp.take_along_axis(weights, level + lane, axis=1)
                mixing = (weight * jnp.exp(jnp.minimum(exponent, 0.0)) * scores).astype(BF16)
                col = slice(h * CHUNK, (h + 1) * CHUNK)
                acc[at, col] = dot(mixing, vals[at, col])

        if t == 0:
            @pl.when(section % 2 == 0)
            def _():
                for c in range(chunks):
                    near(c)

        decay = wide[inner_bits, 0]
        for p in range(pieces):
            cols = slice(p * pair, (p + 1) * pair)
            group = [parts[c * CHUNK : (c + 1) * CHUNK, cols] for c in range(chunks)]
            slot = 0
            for e in range(inner_bits):
                merged = []
                for g in range(0, len(group), 2):
                    inner[slot * n : (slot + 1) * n, cols] = group[g].astype(BF16)
                    slot += 1
                    merged.append(
                        group[g] * jnp.exp(wide[e, g + 1][:, cols]) + group[g + 1]
                    )
                group = merged
            subtree[:, cols] = group[0]
            put(0, p, decay[:, cols])

        def add_level(at, coef, l, state):
            far = dot(qk[at, n:], state)
            for h in range(heads):
                col = slice(h * CHUNK, (h + 1) * CHUNK)
                acc[at, col] += coef[:, h * SLOT + l : h * SLOT + l + 1] * far[:, col]

        def near_states(c):
            at = slice(c * CHUNK, (c + 1) * CHUNK)
            for slot, (e, g) in enumerate(slots):
                if c >> e != g:
                    continue
                prefix = sum(totals[g << e : c], jnp.zeros_like(totals[0]))
                coef = lw_ref[at, :] * jnp.exp(local[at, :] + prefix)
                add_level(at, coef, base + e + 1, inner[slot * n : (slot + 1) * n, :])

        def far_state(d, prefix):
            factor = jnp.where(bit_of(d) == 1, jnp.exp(prefix), 0.0)
            return jnp.concatenate(
                [
                    (recv[t, d, p, :n, :].astype(F32) * factor[:, p * pair : (p + 1) * pair]).astype(BF16)
                    for p in range(pieces)
                ],
                axis=1,
            )

        def distant(c, d, state):
            at = slice(c * CHUNK, (c + 1) * CHUNK)
            before = sum(totals[:c], jnp.zeros_like(totals[0]))
            coef = lw_ref[at, :] * jnp.exp(local[at, :] + before)
            add_level(at, coef, tok_bits + 1 + d, state)

        def near_late(c):
            pl.when(section % 2 == 1)(functools.partial(near, c))

        work = [functools.partial(near_late if t == 0 else near, c) for c in range(chunks)]
        work += [functools.partial(near_states, c) for c in range(1, chunks)]
        prefix = jnp.zeros_like(decay)
        prefixes = []
        taken = 0
        for d in range(bits):
            stop = len(work) * (2 * d + 2) // (2 * bits) if d < bits - 1 else len(work)
            for item in work[taken:stop]:
                item()
            taken = stop
            if d >= 2:
                for e in range(d - 2, d) if d == bits - 1 else (d - 2,):
                    state = far_state(e, prefixes[e])
                    for c in range(chunks):
                        distant(c, e, state)
            upper = bit_of(d) == 1
            prefixes.append(prefix)
            found = []
            for p in range(pieces):
                cols = slice(p * pair, (p + 1) * pair)
                exchange(t, d, p).wait()
                if d == bits - 1:
                    continue
                tail = recv[t, d, p, n:, :].astype(F32)
                there = tail[0:1, :] + tail[1:2, :] + tail[2:3, :]
                here = decay[:, cols]
                mine = jnp.exp(jnp.where(upper, 0.0, there))
                theirs = jnp.exp(jnp.where(upper, here, 0.0))
                subtree[:, cols] = subtree[:, cols] * mine + recv[t, d, p, :n, :].astype(F32) * theirs
                found.append(there)
                put(d + 1, p, here + there)
            if d < bits - 1:
                there = jnp.concatenate(found, axis=1)
                prefix = jnp.where(upper, prefix + there, prefix)
                decay = decay + there
        rest = range(bits - 1, bits) if bits >= 3 else range(bits)
        states = [(d, far_state(d, prefixes[d])) for d in rest]
        if t == 0:
            loads[2].wait()
        for c in range(chunks):
            at = slice(c * CHUNK, (c + 1) * CHUNK)
            for d, state in states:
                distant(c, d, state)
            mixed = acc[at, :]
            scale = lax.rsqrt(jnp.mean(mixed * mixed, axis=-1, keepdims=True) + EPSILON)
            nmix[at, :] = (mixed * scale * out_gain_ref[...]).astype(BF16)
            if t == 0:

                @pl.loop(0, width // (2 * CHUNK))
                def _(i):
                    col = pl.ds(pl.multiple_of(i * 2 * CHUNK, 2 * CHUNK), 2 * CHUNK)
                    handed[at, col] = (
                        x_ref[at, col].astype(F32) + dot(nmix[at, :], wo_ref[:, col])
                    ).astype(BF16)

                handoff(c).start()

    tick(0)
    tick(1)
    keep = pltpu.make_async_copy(arrived, arrived_hbm, load_sem.at[0])
    keep.start()
    for c in range(chunks):
        handoff(c).wait_send()
    keep.wait()


def out_kernel(mix_ref, x_ref, wo_ref, y_ref):
    y_ref[...] = (x_ref[...].astype(F32) + dot(mix_ref[...], wo_ref[...])).astype(BF16)


def body(
    activations,
    norm_gain,
    value_weight,
    shared_weight,
    rate_weight,
    rate_bias,
    decay_rate,
    level_table,
    level_ids,
    out_gain,
    out_weight,
):
    rows, width = activations.shape[1:]
    heads = rate_bias.shape[1]
    buckets, levels = level_table.shape[1:3]
    inner_width = value_weight.shape[2]
    tok_bits = rows.bit_length() - 1
    bits = lax.axis_size("seq").bit_length() - 1
    chunks = rows // CHUNK
    pieces = heads // 2
    table = jnp.transpose(level_table[0], (1, 0, 2))
    table = jnp.pad(table, ((0, SLOT - levels), (0, SLOT - buckets), (0, 0)))
    table = table.reshape(SLOT * SLOT, heads)
    ids = level_ids[0].T
    hbm = pl.BlockSpec(memory_space=pl.ANY)
    near = pl.BlockSpec(memory_space=pltpu.VMEM)
    states = (2, bits, pieces, CHUNK + SLOT, inner_width // pieces)
    normed_mix, arrived = pl.pallas_call(
        functools.partial(ticks_kernel, heads, bits, tok_bits, pieces),
        out_shape=(
            jax.ShapeDtypeStruct((rows, inner_width), BF16),
            jax.ShapeDtypeStruct((rows, width), BF16),
        ),
        in_specs=[near, near, hbm, hbm, near, near, near, near, near, near, hbm],
        out_specs=(near, hbm),
        scratch_shapes=[
            pltpu.VMEM(value_weight.shape[1:], BF16),
            pltpu.VMEM(shared_weight.shape[1:], BF16),
            pltpu.VMEM(out_weight.shape[1:], BF16),
            pltpu.VMEM((rows, heads * SLOT), F32),
            pltpu.VMEM((rows, width), BF16),
            pltpu.VMEM((rows, heads * SLOT), F32),
            pltpu.VMEM((rows, heads * SLOT), F32),
            pltpu.VMEM((rows, inner_width), BF16),
            pltpu.VMEM((rows, shared_weight.shape[2]), BF16),
            pltpu.VMEM((rows, inner_width), F32),
            pltpu.VMEM((rows, inner_width), F32),
            pltpu.VMEM((max(chunks - 1, 1) * CHUNK, inner_width), BF16),
            pltpu.VMEM((CHUNK, inner_width), F32),
            pltpu.VMEM((chunks, 8, heads * SLOT), F32),
            pltpu.VMEM((rows, width), BF16),
            pltpu.VMEM((rows, width), BF16),
            pltpu.VMEM(states, BF16),
            pltpu.VMEM(states, BF16),
            pltpu.SemaphoreType.DMA((3,)),
            pltpu.SemaphoreType.DMA(states[:3]),
            pltpu.SemaphoreType.DMA(states[:3]),
            pltpu.SemaphoreType.DMA((chunks,)),
            pltpu.SemaphoreType.DMA((chunks,)),
        ],
        compiler_params=pltpu.CompilerParams(
            collective_id=0, has_side_effects=True, vmem_limit_bytes=56 * 1024 * 1024
        ),
    )(
        activations[0],
        norm_gain,
        value_weight[0],
        shared_weight[0],
        rate_weight[0].T,
        rate_bias,
        decay_rate,
        table,
        ids,
        out_gain,
        out_weight[0],
    )
    tile = 2 * CHUNK
    column = pl.BlockSpec((rows, tile), lambda i: (0, i))
    return pl.pallas_call(
        out_kernel,
        grid=(width // tile,),
        out_shape=jax.ShapeDtypeStruct((rows, width), BF16),
        in_specs=[
            pl.BlockSpec((rows, inner_width), lambda i: (0, 0)),
            column,
            pl.BlockSpec((inner_width, tile), lambda i: (0, i)),
        ],
        out_specs=column,
    )(normed_mix, arrived, out_weight[0])[None]


def solution(mesh):
    placed = (
        P("section", "seq", None),
        P("section", None),
        P("section", None, None),
        P("section", None, None),
        P("section", None, None),
        P("section", None),
        P("section", None),
        P("section", None, None, None),
        P("section", "seq", None),
        P("section", None),
        P("section", None, None),
    )
    return jax.shard_map(
        body, mesh=mesh, in_specs=placed, out_specs=P("section", "seq", None), check_vma=False
    )
```
